1024 devices in a mesh: band: 16 (over x, y_lo, core), slab: 64 (over z, y_hi).
Axes of the slice: x: 4, y: 4 (y_hi: 2, y_lo: 2; y = y_hi * 2 + y_lo), z: 32, core: 2. Of those that a mesh axis runs over, the one named last changes fastest.
Arguments:
- orbitals: float32 [64, 128, 128, 128], P('band', 'slab'), may hold values from -6 to 6
- occupations: float32 [64], P('band'), may hold values from 0.1 to 1
- accumulated: float32 [64, 128, 128, 128], P('band', 'slab'), may hold values from -6 to 6
Outputs:
- exchange_terms: float32 [64, 128, 128, 128], P('band', 'slab')
The draws below stay inside these ranges and needn't reach their ends.
All inputs are finite; a program needn't handle non-finite values.
Results may differ from the reference program's by a relative error of at most 0.00012.
Values sent between devices are 32-bit elements; how exact they have to be, the bound alone decides.
A program may use at most 32 MiB of HBM per device.

```python
import math
import jax
import jax.numpy as jnp
from jax import lax

GRID = 128
ORB_DEV = 4
HOPS = 3
ORBITALS = 64
N_BAND = 16


def shard_levels(own_key, shape, shards, smallest, top_value):
    loudness, own = 1.0, jax.random.fold_in(own_key, 6)
    for dim, shards_of in shards:
        draws = jnp.exp(jax.random.uniform(jax.random.fold_in(own, dim), (shards_of,), jnp.float32, smallest / len(shards), top_value / len(shards)))
        loudness = loudness * jnp.repeat(draws, shape[dim] // shards_of).reshape([-1 if axis == dim else 1 for axis in range(len(shape))])
    return loudness


def bell_draw(rng, extent, width, reach, shards=(), kind=jnp.bfloat16):
    drawn = jax.random.normal(rng, extent, jnp.float32) * width
    if len(shards) > 0:
        drawn = shard_levels(rng, extent, shards, -0.22, 0.18) * drawn
    return jnp.clip(drawn, min=-reach, max=reach).astype(kind)


def setup_inputs(seed: int = 0) -> dict:
    seeds = jax.random.split(jax.random.key(seed), 4)
    return {
        "orbitals": bell_draw(seeds[0], (ORBITALS, GRID, GRID, GRID), 1.0, 6.0, ((0, 16), (1, 64)), jnp.float32),
        "occupations": jnp.clip(jnp.exp(math.log(1.0) - 2.3025851 * jax.random.uniform(seeds[1], (ORBITALS,), jnp.float32) ** shard_levels(seeds[1], (ORBITALS,), ((0, 16),), -0.2, 0.2)), 0.1, 1.0),
        "accumulated": bell_draw(seeds[2], (ORBITALS, GRID, GRID, GRID), 1.0, 6.0, ((0, 16), (1, 64)), jnp.float32),
    }


def kernel_grid():
    index = jnp.arange(GRID, dtype=jnp.int32)
    signed = jnp.where(index < GRID // 2, index, index - GRID)
    wave = signed.astype(jnp.float32) * (2.0 * math.pi / GRID)
    square = wave[:, None, None] ** 2 + wave[None, :, None] ** 2 + wave[None, None, :] ** 2
    return 4.0 * math.pi / (square + 0.01)


def reference(orbitals, occupations, accumulated):
    screening = kernel_grid()
    visitors = orbitals[::ORB_DEV]
    visitor_occ = occupations[::ORB_DEV]
    owner = jnp.arange(ORBITALS, dtype=jnp.int32) // ORB_DEV
    result = accumulated
    for travel in range(1, HOPS + 1):
        source = ((owner - travel) % N_BAND).astype(jnp.int32)

        def pair_term(items):
            resident, which = items
            visitor = visitors[which]
            spectrum = jnp.fft.fftn(resident * visitor)
            potential = jnp.real(jnp.fft.ifftn(screening * spectrum)).astype(resident.dtype)
            return visitor_occ[which] * visitor * potential

        result = result - lax.map(pair_term, (orbitals, source))
    return result
```

```python
import functools
import math

import jax
import jax.numpy as jnp
import ml_dtypes
import numpy as np
from jax import lax
from jax.experimental import pallas as pl
from jax.experimental.pallas import tpu as pltpu
from jax.sharding import PartitionSpec as P

MESH = pl.DeviceIdType.MESH
F32 = jnp.float32
BF16 = jnp.bfloat16
SUB = 8

(
    IN_PV, IN_PR0, IN_PR1, IN_OCC, IN_CV, IN_R, IN_VD, IN_VF, IN_T, IN_U, IN_Q, IN_RET, N_IN
) = (0, 1, 2, 3, 4, 5, 6, 9, 12, 15, 18, 19, 20)


def hartley(extent):
    index = np.arange(extent)
    angle = (index[:, None] * index[None, :] % extent) * (2.0 * math.pi / extent)
    full = np.cos(angle) + np.sin(angle)
    high = full.astype(ml_dtypes.bfloat16)
    low = (full - high.astype(np.float64)).astype(ml_dtypes.bfloat16)
    return high, low


def split(value):
    high = value.astype(BF16)
    low = (value - high.astype(F32)).astype(BF16)
    return high, low


def rows_times(value, matrix):
    n = value.shape[1]
    both = jnp.concatenate(split(value), axis=1)
    out = jnp.dot(both, matrix, preferred_element_type=F32)
    return out[:, :n] + out[:, n:]


def times_columns(matrix, value):
    n = value.shape[0]
    both = jnp.concatenate(split(value), axis=0)
    out = jnp.dot(matrix, both, preferred_element_type=F32)
    return out[:n] + out[n:]


def kernel(
    bands, extent,
    orb, occ, acc, right_mat, left_mat, out,
    pv, pr0, pr1, occ_own, occ_all, cv, res, vis, mid, fwd, tin, tout, back, done, ret_z, ret,
    send_sem, in_sem,
):
    nz, nw = 2 * bands, bands
    b, s = lax.axis_index("band"), lax.axis_index("slab")
    z, yh, g = s // 2, s % 2, b % 2
    w = (b // 2) * 2 + yh
    place = 2 * w + g

    def device(tw, tg, tz):
        return {"band": (tw // 2) * 2 + tg, "slab": 2 * tz + tw % 2}

    def push(src, dst, sem, target):
        pltpu.make_async_remote_copy(
            src_ref=src, dst_ref=dst, send_sem=send_sem.at[sem], recv_sem=in_sem.at[sem],
            device_id=target, device_id_type=MESH,
        ).start()

    def keep(src, dst, sem):
        pltpu.make_async_copy(src, dst, in_sem.at[sem]).start()

    def arrived(ref, sem):
        pltpu.make_async_copy(ref, ref, in_sem.at[sem]).wait()

    def sent(ref, sem):
        pltpu.make_async_copy(ref, ref, send_sem.at[sem]).wait()

    def loop(low, high, fn):
        def step(i, carry):
            fn(i)
            return carry
        lax.fori_loop(low, high, step, 0)

    occ_own[...] = jnp.full(occ_own.shape, occ[0], F32)

    barrier = pltpu.get_barrier_semaphore()

    def greet(target):
        pl.semaphore_signal(barrier, inc=1, device_id=target, device_id_type=MESH)

    def greet_plane(d):
        t = (place + d) % (2 * nw)
        greet(device(t // 2, t % 2, z))

    loop(1, nz, lambda d: greet(device(w, g, (z + d) % nz)))
    loop(1, 2 * nw, greet_plane)

    @pl.when(g == 0)
    def _():
        greet(device(w, 1, (z + 3) % nz))

    pl.semaphore_wait(barrier, 2 * nw - 1 + nz - 1 + g)

    mine = 2 * b + yh

    def visitors_out(d):
        t = (place + d) % (2 * nw)
        push(orb.at[0, t % 2, t // 2], pv.at[mine], IN_PV, device(t // 2, t % 2, z))

    def residents_out(d):
        t = (place + d) % (2 * nw)
        tw, tg = t // 2, t % 2
        push(orb.at[2 + tg, :, tw], pr0.at[mine], IN_PR0, device(tw, tg, z))

    def seconds_out(d):
        tw = (w + d) % nw
        push(orb.at[1, :, tw], pr1.at[mine], IN_PR1, device(tw, 1, z))

    def weights_out(d):
        t = (place + d) % (2 * nw)
        tw, tg = t // 2, t % 2

        @pl.when(tw % 2 == yh)
        def _():
            push(occ_own, occ_all.at[b], IN_OCC, device(tw, tg, z))

    loop(1, 2 * nw, visitors_out)
    keep(orb.at[0, g, w], pv.at[mine], IN_PV)
    loop(1, 2 * nw, residents_out)
    keep(orb.at[2 + g, :, w], pr0.at[mine], IN_PR0)
    loop(1, nw, seconds_out)

    @pl.when(g == 0)
    def _():
        push(orb.at[1, :, w], pr1.at[mine], IN_PR1, device(w, 1, z))

    @pl.when(g == 1)
    def _():
        keep(orb.at[1, :, w], pr1.at[mine], IN_PR1)

    loop(1, 2 * nw, weights_out)
    keep(occ_own, occ_all.at[b], IN_OCC)

    half = bands // 2

    def signed(m):
        reach = half - (m + 1) // 2
        return jnp.where(m % 2 == 0, reach, -reach)

    def centre_out(m):
        tz = (z // 2 * 2 + 2 * signed(m) + nz) % nz
        owner = (tz // 2 - 2 + bands) % bands
        src, dst = pv.at[pl.ds(2 * owner, 2)], cv.at[pl.ds(2 * z, 2)]

        @pl.when(tz == z)
        def _():
            keep(src, dst, IN_CV)

        @pl.when(tz != z)
        def _():
            push(src, dst, IN_CV, device(w, g, tz))

    def home_out(m, stage, odd):
        tz = (z // 2 * 2 + 2 * signed(m) + odd + nz) % nz
        owner = tz // 2
        src, dst = stage.at[pl.ds(2 * owner, 2)], res.at[pl.ds(2 * z, 2)]

        @pl.when(tz == z)
        def _():
            keep(src, dst, IN_R)

        @pl.when(tz != z)
        def _():
            push(src, dst, IN_R, device(w, g, tz))

    arrived(pv, IN_PV)
    loop(0, bands, centre_out)
    arrived(pr0, IN_PR0)
    loop(0, bands, lambda m: home_out(m, pr0, 0))

    @pl.when(g == 1)
    def _():
        arrived(pr1, IN_PR1)
        loop(0, bands, lambda m: home_out(m, pr1, 1))

    @pl.when(z % 2 == 0)
    def _():
        arrived(cv, IN_CV)
        keep(cv, vis.at[1, :, g], IN_VD + 1)
        for d, h in ((1, 1), (-1, 0), (-2, 0), (2, 2), (3, 2)):
            push(cv, vis.at[h, :, g], IN_VD + h, device(w, g, (z + d + nz) % nz))
        push(cv, res.at[:, g], IN_R, device(w, 0, (z - 3 + nz) % nz))

    order = (1, 0, 2)

    def share(h):
        half_vis = vis.at[h, :, g]
        arrived(half_vis, IN_VD + h)
        push(half_vis, half_vis, IN_VF + h, device(w, 1 - g, z))

    def transform_x(src, dst):
        for y in range(0, SUB, 2):
            two = jnp.concatenate(
                [src[pl.ds(y + k, extent, stride=SUB), :] for k in range(2)], axis=1
            )
            two = times_columns(left_mat[...], two)
            for k in range(2):
                dst[pl.ds(y + k, extent, stride=SUB), :] = two[:, k * extent:(k + 1) * extent]

    rows = extent * SUB
    slab_rows = SUB * SUB
    for h in order:
        share(h)
    arrived(res, IN_R)
    for h in order:
        arrived(vis.at[h, :, 1 - g], IN_VF + h)
        pair = (res[...] * vis[h]).reshape(rows, extent)
        mid[...] = rows_times(pair, right_mat[...])
        transform_x(mid, fwd.at[h])

        def fwd_out(d, h=h):
            tw = (w + d) % nw
            push(fwd.at[h, pl.ds(slab_rows * tw, slab_rows)], tin.at[h, w], IN_T + h, device(tw, g, z))

        loop(1, nw, fwd_out)
        keep(fwd.at[h, pl.ds(slab_rows * w, slab_rows)], tin.at[h, w], IN_T + h)

    def wave(index):
        near = jnp.where(index < extent // 2, index, index - extent)
        return near.astype(F32) * (2.0 * math.pi / extent)

    shape = (extent, extent)
    square = (
        wave(lax.broadcasted_iota(jnp.int32, shape, 0)) ** 2
        + wave(lax.broadcasted_iota(jnp.int32, shape, 1)) ** 2
    )

    def screening(a):
        index = SUB * w + a
        return (4.0 * math.pi / float(extent**3)) / (square + wave(index) ** 2 + 0.01)

    for h in order:
        arrived(tin.at[h], IN_T + h)
        for a in range(0, SUB, 2):
            two = jnp.concatenate(
                [tin[h, :, SUB * (a + k):SUB * (a + k + 1), :].reshape(shape) for k in range(2)],
                axis=1,
            )
            two = times_columns(left_mat[...], two)
            two = two * jnp.concatenate([screening(a), screening(a + 1)], axis=1)
            two = times_columns(left_mat[...], two)
            for k in range(2):
                tout[h, :, SUB * (a + k):SUB * (a + k + 1), :] = two[
                    :, k * extent:(k + 1) * extent
                ].reshape(nw, SUB, extent)

        def back_out(d, h=h):
            tw = (w + d) % nw
            push(tout.at[h, tw], back.at[h, pl.ds(slab_rows * w, slab_rows)], IN_U + h, device(tw, g, z))

        loop(1, nw, back_out)
        keep(tout.at[h, w], back.at[h, pl.ds(slab_rows * w, slab_rows)], IN_U + h)

    arrived(occ_all, IN_OCC)
    for h in order:
        arrived(back.at[h], IN_U + h)
        transform_x(back.at[h], mid)
        potential = rows_times(mid[...], right_mat[...]).reshape(extent // 2, 2, SUB, extent)
        owner = (z // 2 - (h + 1) + bands) % bands
        term = vis[h] * potential * occ_all[owner][None, None]
        term = term.reshape(done.shape)
        if h == order[0]:
            done[...] = term
        else:
            done[...] += term

    def slabs_out(m):
        reach = nz // 2 - m // 2
        tz = (z + jnp.where(m % 2 == 1, reach, nz - reach)) % nz
        push(done.at[tz], ret_z.at[z // 2, z % 2], IN_Q, device(w, g, tz))

    loop(1, nz, slabs_out)
    keep(done.at[z], ret_z.at[z // 2, z % 2], IN_Q)
    arrived(ret_z, IN_Q)

    def owners_out(d):
        t = (place + d) % (2 * nw)
        tw, tg = t // 2, t % 2
        owner = (tw // 2) * 2 + tg
        push(ret_z.at[owner, :, tw % 2], ret.at[:, g, :, w], IN_RET, device(tw, tg, z))

    loop(1, 2 * nw, owners_out)
    keep(ret_z.at[b, :, yh], ret.at[:, g, :, w], IN_RET)
    arrived(ret, IN_RET)
    for first in range(2):
        for core in range(2):
            j = 2 * (1 - first) + core
            out[j] = acc[j] - ret[first, core]

    sent(pv.at[pl.ds(1, 2 * nw - 1)], IN_PV)
    sent(pr0.at[pl.ds(1, 2 * nw - 1)], IN_PR0)
    sent(pr1.at[pl.ds(0, nw - 1)], IN_PR1)

    @pl.when(g == 0)
    def _():
        sent(pr1.at[0], IN_PR1)

    sent(occ_all.at[pl.ds(0, nw - 1)], IN_OCC)
    sent(cv.at[pl.ds(0, 2 * bands - 2)], IN_CV)
    sent(res.at[pl.ds(0, 2 * bands - 2)], IN_R)

    @pl.when(z % 2 == 1)
    def _():
        sent(cv.at[pl.ds(0, 2)], IN_CV)
        sent(res.at[pl.ds(0, 2)], IN_R)

    @pl.when(g == 1)
    def _():
        sent(res.at[pl.ds(0, 2 * bands - 2)], IN_R)

    @pl.when(jnp.logical_and(g == 1, z % 2 == 0))
    def _():
        sent(res.at[pl.ds(0, 2)], IN_R)

    @pl.when(z % 2 == 0)
    def _():
        sent(res.at[:, g], IN_R)
        for h in (1, 0, 0, 2, 2):
            sent(cv, IN_VD + h)

    for h in order:
        sent(vis.at[h, :, g], IN_VF + h)
        sent(tin.at[h, pl.ds(0, nw - 1)], IN_T + h)
        sent(tout.at[h, pl.ds(0, nw - 1)], IN_U + h)
    sent(done.at[pl.ds(0, nz - 1)], IN_Q)
    sent(done.at[pl.ds(0, 2 * nw - 1)], IN_RET)


def body(orbitals, occupations, accumulated):
    extent = orbitals.shape[2]
    bands = lax.axis_size("band")
    nz, nw = 2 * bands, bands
    high, low = hartley(extent)
    right_mat = jnp.asarray(np.block([[high, low], [high, low]]))
    left_mat = jnp.asarray(np.block([[high, high], [low, low]]))
    tiled = (orbitals.shape[0], orbitals.shape[1], nw, SUB, extent)
    rows = extent * SUB
    tile = (SUB, extent)
    vmem = pl.BlockSpec(memory_space=pltpu.VMEM)
    scratch = [
        (2 * bands, *tile),
        (2 * bands, 2, *tile),
        (2 * bands, 2, *tile),
        tile,
        (bands, *tile),
        (2 * nz, *tile),
        (2 * nz, 2, *tile),
        (3, 2 * nz, 2, *tile),
        (rows, extent),
        (3, rows, extent),
        (3, nw, SUB * SUB, extent),
        (3, nw, SUB * SUB, extent),
        (3, rows, extent),
        (nz, 2, 2, *tile),
        (bands, 2, 2, 2, *tile),
        (2, 2, 2, nw, *tile),
    ]
    result = pl.pallas_call(
        functools.partial(kernel, bands, extent),
        out_shape=jax.ShapeDtypeStruct(tiled, F32),
        in_specs=[vmem, pl.BlockSpec(memory_space=pltpu.SMEM), vmem, vmem, vmem],
        out_specs=vmem,
        scratch_shapes=[pltpu.VMEM(shape, F32) for shape in scratch]
        + [pltpu.SemaphoreType.DMA((N_IN,)), pltpu.SemaphoreType.DMA((N_IN,))],
        compiler_params=pltpu.CompilerParams(
            collective_id=0, has_side_effects=True, vmem_limit_bytes=40 * 2**20
        ),
    )(orbitals.reshape(tiled), occupations, accumulated.reshape(tiled), right_mat, left_mat)
    return result.reshape(orbitals.shape)


def solution(mesh):
    in_specs = (P("band", "slab", None, None), P("band"), P("band", "slab", None, None))
    out_specs = P("band", "slab", None, None)
    return jax.shard_map(body, mesh=mesh, in_specs=in_specs, out_specs=out_specs, check_vma=False)
```

```python
import functools
import math

import jax
import jax.numpy as jnp
import ml_dtypes
import numpy as np
from jax import lax
from jax.experimental import pallas as pl
from jax.experimental.pallas import tpu as pltpu
from jax.sharding import PartitionSpec as P

MESH = pl.DeviceIdType.MESH
F32 = jnp.float32
BF16 = jnp.bfloat16
SUB = 8

CHUNKS = 4

IN_PV, IN_PR0, IN_PR1, IN_OCC, IN_CV, IN_R = range(6)
IN_VF, IN_T, IN_U, IN_RET, IN_Q, IN_ACC, IN_MAT, OUT_CHAIN = 6, 9, 12, 15, 17, 18, 19, 20
IN_VD = 21
N_SEM = IN_VD + 3 * CHUNKS


def hartley(extent):
    index = np.arange(extent)
    angle = (index[:, None] * index[None, :] % extent) * (2.0 * math.pi / extent)
    full = np.cos(angle) + np.sin(angle)
    high = full.astype(ml_dtypes.bfloat16)
    low = (full - high.astype(np.float64)).astype(ml_dtypes.bfloat16)
    return high, low


def split(value):
    high = value.astype(BF16)
    low = (value - high.astype(F32)).astype(BF16)
    return high, low


def rows_times(value, matrix):
    n = value.shape[1]
    both = jnp.concatenate(split(value), axis=1)
    out = jnp.dot(both, matrix, preferred_element_type=F32)
    return out[:, :n] + out[:, n:]


def times_columns(matrix, value):
    n = value.shape[0]
    both = jnp.concatenate(split(value), axis=0)
    out = jnp.dot(matrix, both, preferred_element_type=F32)
    return out[:n] + out[n:]


def kernel(
    bands, extent,
    orb, occ, acc_hbm, right_hbm, left_hbm, out,
    acc, right_mat, left_mat, pv, pr0, pr1, occ_own, occ_all, cv, res, vis, mid, fwd, tin, tout, back, done, ret_z, ret,
    send_sem, in_sem, turn,
):
    nz, nw = 2 * bands, bands
    b, s = lax.axis_index("band"), lax.axis_index("slab")
    z, yh, g = s // 2, s % 2, b % 2
    w = (b // 2) * 2 + yh
    place = 2 * w + g

    def device(tw, tg, tz):
        return {"band": (tw // 2) * 2 + tg, "slab": 2 * tz + tw % 2}

    def push(src, dst, sem, target, leave=None):
        pltpu.make_async_remote_copy(
            src_ref=src, dst_ref=dst, recv_sem=in_sem.at[sem],
            send_sem=send_sem.at[sem if leave is None else leave],
            device_id=target, device_id_type=MESH,
        ).start()

    def keep(src, dst, sem):
        pltpu.make_async_copy(src, dst, in_sem.at[sem]).start()

    def arrived(ref, sem):
        pltpu.make_async_copy(ref, ref, in_sem.at[sem]).wait()

    def sent(ref, sem):
        pltpu.make_async_copy(ref, ref, send_sem.at[sem]).wait()

    def loop(low, high, fn):
        def step(i, carry):
            fn(i)
            return carry
        lax.fori_loop(low, high, step, 0)

    keep(acc_hbm, acc, IN_ACC)
    keep(right_hbm, right_mat, IN_MAT)
    keep(left_hbm, left_mat, IN_MAT)
    occ_own[...] = jnp.full(occ_own.shape, occ[0], F32)

    barrier = pltpu.get_barrier_semaphore()

    def greet(target):
        pl.semaphore_signal(barrier, inc=1, device_id=target, device_id_type=MESH)

    def greet_plane(d):
        t = (place + d) % (2 * nw)
        greet(device(t // 2, t % 2, z))

    loop(1, nz, lambda d: greet(device(w, g, (z + d) % nz)))
    loop(1, 2 * nw, greet_plane)

    @pl.when(g == 0)
    def _():
        greet(device(w, 1, (z + 1) % nz))

    pl.semaphore_wait(barrier, 2 * nw - 1 + nz - 1 + g)

    mine = 2 * b + yh

    def visitors_out(d):
        t = (place + d) % (2 * nw)
        push(orb.at[0, t % 2, t // 2], pv.at[mine], IN_PV, device(t // 2, t % 2, z))

    def residents_out(d):
        t = (place + d) % (2 * nw)
        tw, tg = t // 2, t % 2
        push(orb.at[2 + tg, :, tw], pr0.at[mine], IN_PR0, device(tw, tg, z))

    def seconds_out(d):
        tw = (w + d) % nw
        push(orb.at[1, :, tw], pr1.at[mine], IN_PR1, device(tw, 1, z))

    def weights_out(d):
        t = (place + d) % (2 * nw)
        tw, tg = t // 2, t % 2

        @pl.when(tw % 2 == yh)
        def _():
            push(occ_own, occ_all.at[b], IN_OCC, device(tw, tg, z))

    loop(1, 2 * nw, visitors_out)
    keep(orb.at[0, g, w], pv.at[mine], IN_PV)
    loop(1, 2 * nw, residents_out)
    keep(orb.at[2 + g, :, w], pr0.at[mine], IN_PR0)

    half = bands // 2

    def signed(m):
        reach = half - (m + 1) // 2
        return jnp.where(m % 2 == 0, reach, -reach)

    def centre_out(m):
        tz = (z // 2 * 2 + 2 * signed(m) + nz) % nz
        owner = (tz // 2 - 2 + bands) % bands
        src, dst = pv.at[pl.ds(2 * owner, 2)], cv.at[pl.ds(2 * z, 2)]

        @pl.when(tz == z)
        def _():
            keep(src, dst, IN_CV)

        @pl.when(tz != z)
        def _():
            push(src, dst, IN_CV, device(w, g, tz))

    def home_out(m, stage, odd):
        tz = (z // 2 * 2 + 2 * signed(m) + odd + nz) % nz
        owner = tz // 2
        src, dst = stage.at[pl.ds(2 * owner, 2)], res.at[pl.ds(2 * z, 2)]

        @pl.when(tz == z)
        def _():
            keep(src, dst, IN_R)

        @pl.when(tz != z)
        def _():
            push(src, dst, IN_R, device(w, g, tz))

    arrived(pv, IN_PV)
    loop(0, bands, centre_out)

    loop(1, nw, seconds_out)

    @pl.when(g == 0)
    def _():
        push(orb.at[1, :, w], pr1.at[mine], IN_PR1, device(w, 1, z))

    @pl.when(g == 1)
    def _():
        keep(orb.at[1, :, w], pr1.at[mine], IN_PR1)

    loop(1, 2 * nw, weights_out)
    keep(occ_own, occ_all.at[b], IN_OCC)

    even = z % 2 == 0
    above, below = device(w, g, (z + 1) % nz), device(w, g, (z - 1 + nz) % nz)
    piece = 2 * nz // CHUNKS

    def visitor(h, k):
        return vis.at[h, pl.ds(piece * k, piece), g]

    def pass_on(src, h, k, target):
        push(src, visitor(h, k), IN_VD + CHUNKS * h + k, target, OUT_CHAIN)

    def came(h, k):
        arrived(visitor(h, k), IN_VD + CHUNKS * h + k)

    sent(pv.at[pl.ds(0, 2 * bands - 2)], IN_CV)

    @pl.when(even)
    def _():
        arrived(cv, IN_CV)
        for k in range(CHUNKS):
            part = cv.at[pl.ds(piece * k, piece)]
            pass_on(part, 1, k, above)
            pass_on(part, 0, k, below)
        for k in range(CHUNKS):
            keep(cv.at[pl.ds(piece * k, piece)], visitor(1, k), IN_VD + CHUNKS + k)

    @pl.when(jnp.logical_not(even))
    def _():
        sent(pv.at[pl.ds(0, 2)], IN_CV)

    @pl.when(even)
    def _():
        for k in range(CHUNKS):
            came(0, k)
            push(
                visitor(0, k), res.at[pl.ds(piece * k, piece), g], IN_R,
                device(w, 0, (z - 1 + nz) % nz), OUT_CHAIN,
            )
            came(2, k)
            pass_on(visitor(2, k), 2, k, above)
        for k in range(CHUNKS):
            came(1, k)

    @pl.when(jnp.logical_not(even))
    def _():
        for k in range(CHUNKS):
            came(0, k)
            pass_on(visitor(0, k), 0, k, below)
            came(1, k)
            pass_on(visitor(1, k), 2, k, above)

    @pl.when(g == 0)
    def _():
        arrived(pr0, IN_PR0)
        loop(0, bands, lambda m: home_out(m, pr0, 0))

    @pl.when(jnp.logical_not(even))
    def _():
        for k in range(CHUNKS):
            came(2, k)

    order = (1, 0, 2)

    def share(h):
        half_vis = vis.at[h, :, g]
        push(half_vis, half_vis, IN_VF + h, device(w, 1 - g, z))

    def transform_x(src, dst):
        for y in range(0, SUB, 2):
            two = jnp.concatenate(
                [src[pl.ds(y + k, extent, stride=SUB), :] for k in range(2)], axis=1
            )
            two = times_columns(left_mat[...], two)
            for k in range(2):
                dst[pl.ds(y + k, extent, stride=SUB), :] = two[:, k * extent:(k + 1) * extent]

    rows = extent * SUB
    slab_rows = SUB * SUB
    for h in order:
        share(h)

    @pl.when(g == 0)
    def _():
        sent(res.at[pl.ds(0, 2 * bands - 2)], IN_R)

        @pl.when(jnp.logical_not(even))
        def _():
            sent(res.at[pl.ds(0, 2)], IN_R)

        pl.semaphore_signal(turn, inc=1, device_id=device(w, 1, z), device_id_type=MESH)

    @pl.when(g == 1)
    def _():
        arrived(pr0, IN_PR0)
        arrived(pr1, IN_PR1)
        pl.semaphore_wait(turn, 1)

        def both(m):
            home_out(m, pr0, 0)
            home_out(m, pr1, 1)

        loop(0, bands, both)

    arrived(right_mat, IN_MAT)
    arrived(left_mat, IN_MAT)
    arrived(res, IN_R)
    for h in order:
        arrived(vis.at[h, :, 1 - g], IN_VF + h)
        pair = (res[...] * vis[h]).reshape(rows, extent)
        mid[...] = rows_times(pair, right_mat[...])
        transform_x(mid, fwd.at[h])

        def fwd_out(d, h=h):
            tw = (w + d) % nw
            push(fwd.at[h, pl.ds(slab_rows * tw, slab_rows)], tin.at[h, w], IN_T + h, device(tw, g, z))

        loop(1, nw, fwd_out)
        keep(fwd.at[h, pl.ds(slab_rows * w, slab_rows)], tin.at[h, w], IN_T + h)

    def wave(index):
        near = jnp.where(index < extent // 2, index, index - extent)
        return near.astype(F32) * (2.0 * math.pi / extent)

    shape = (extent, extent)
    square = (
        wave(lax.broadcasted_iota(jnp.int32, shape, 0)) ** 2
        + wave(lax.broadcasted_iota(jnp.int32, shape, 1)) ** 2
    )

    def screening(a):
        index = SUB * w + a
        return (4.0 * math.pi / float(extent**3)) / (square + wave(index) ** 2 + 0.01)

    for h in order:
        arrived(tin.at[h], IN_T + h)
        for a in range(0, SUB, 2):
            two = jnp.concatenate(
                [tin[h, :, SUB * (a + k):SUB * (a + k + 1), :].reshape(shape) for k in range(2)],
                axis=1,
            )
            two = times_columns(left_mat[...], two)
            two = two * jnp.concatenate([screening(a), screening(a + 1)], axis=1)
            two = times_columns(left_mat[...], two)
            for k in range(2):
                tout[h, :, SUB * (a + k):SUB * (a + k + 1), :] = two[
                    :, k * extent:(k + 1) * extent
                ].reshape(nw, SUB, extent)

        def back_out(d, h=h):
            tw = (w + d) % nw
            push(tout.at[h, tw], back.at[h, pl.ds(slab_rows * w, slab_rows)], IN_U + h, device(tw, g, z))

        loop(1, nw, back_out)
        keep(tout.at[h, w], back.at[h, pl.ds(slab_rows * w, slab_rows)], IN_U + h)

    arrived(occ_all, IN_OCC)
    for h in order:
        arrived(back.at[h], IN_U + h)
        transform_x(back.at[h], mid)
        potential = rows_times(mid[...], right_mat[...]).reshape(extent // 2, 2, SUB, extent)
        owner = (z // 2 - (h + 1) + bands) % bands
        term = vis[h] * potential * occ_all[owner][None, None]
        term = term.reshape(done.shape)
        if h == order[0]:
            done[...] = term
        else:
            done[...] += term

    def slabs_out(m):
        reach = nz // 2 - m // 2
        tz = (z + jnp.where(m % 2 == 1, reach, nz - reach)) % nz
        push(done.at[tz], ret_z.at[z // 2, z % 2], IN_Q, device(w, g, tz))

    loop(1, nz, slabs_out)
    keep(done.at[z], ret_z.at[z // 2, z % 2], IN_Q)
    arrived(ret_z, IN_Q)

    def owners_out(d):
        t = (place + d) % (2 * nw)
        tw, tg = t // 2, t % 2
        owner = (tw // 2) * 2 + tg
        push(ret_z.at[owner, :, tw % 2], ret.at[:, g, :, w], IN_RET + g, device(tw, tg, z), IN_RET)

    loop(1, 2 * nw, owners_out)
    keep(ret_z.at[b, :, yh], ret.at[:, g, :, w], IN_RET + g)
    arrived(acc, IN_ACC)
    for core in range(2):
        arrived(ret.at[:, core], IN_RET + core)
        for first in range(2):
            j = 2 * (1 - first) + core
            out[j] = acc[j] - ret[first, core]

    sent(pv.at[pl.ds(1, 2 * nw - 1)], IN_PV)
    sent(pr0.at[pl.ds(1, 2 * nw - 1)], IN_PR0)
    sent(pr1.at[pl.ds(0, nw - 1)], IN_PR1)

    @pl.when(g == 0)
    def _():
        sent(pr1.at[0], IN_PR1)

    sent(occ_all.at[pl.ds(0, nw - 1)], IN_OCC)

    @pl.when(g == 1)
    def _():
        sent(res.at[pl.ds(0, 2 * bands - 1)], IN_R)
        sent(res.at[pl.ds(0, 2 * bands - 1)], IN_R)

    sent(cv, OUT_CHAIN)
    sent(cv, OUT_CHAIN)

    @pl.when(even)
    def _():
        sent(cv, OUT_CHAIN)
        sent(cv, OUT_CHAIN)

    for h in order:
        sent(vis.at[h, :, g], IN_VF + h)
        sent(tin.at[h, pl.ds(0, nw - 1)], IN_T + h)
        sent(tout.at[h, pl.ds(0, nw - 1)], IN_U + h)
    sent(done.at[pl.ds(0, nz - 1)], IN_Q)
    sent(done.at[pl.ds(0, 2 * nw - 1)], IN_RET)


def body(orbitals, occupations, accumulated):
    extent = orbitals.shape[2]
    bands = lax.axis_size("band")
    nz, nw = 2 * bands, bands
    high, low = hartley(extent)
    right_mat = jnp.asarray(np.block([[high, low], [high, low]]))
    left_mat = jnp.asarray(np.block([[high, high], [low, low]]))
    tiled = (orbitals.shape[0], orbitals.shape[1], nw, SUB, extent)
    rows = extent * SUB
    tile = (SUB, extent)
    vmem = pl.BlockSpec(memory_space=pltpu.VMEM)
    hbm = pl.BlockSpec(memory_space=pltpu.HBM)
    scratch = [
        (2 * bands, *tile),
        (2 * bands, 2, *tile),
        (2 * bands, 2, *tile),
        tile,
        (bands, *tile),
        (2 * nz, *tile),
        (2 * nz, 2, *tile),
        (3, 2 * nz, 2, *tile),
        (rows, extent),
        (3, rows, extent),
        (3, nw, SUB * SUB, extent),
        (3, nw, SUB * SUB, extent),
        (3, rows, extent),
        (nz, 2, 2, *tile),
        (bands, 2, 2, 2, *tile),
        (2, 2, 2, nw, *tile),
    ]
    result = pl.pallas_call(
        functools.partial(kernel, bands, extent),
        out_shape=jax.ShapeDtypeStruct(tiled, F32),
        in_specs=[hbm, pl.BlockSpec(memory_space=pltpu.SMEM), hbm, hbm, hbm],
        out_specs=vmem,
        scratch_shapes=[pltpu.VMEM(tiled, F32)]
        + [pltpu.VMEM((2 * extent, 2 * extent), BF16)] * 2
        + [pltpu.VMEM(shape, F32) for shape in scratch]
        + [pltpu.SemaphoreType.DMA((N_SEM,))] * 2
        + [pltpu.SemaphoreType.REGULAR],
        compiler_params=pltpu.CompilerParams(
            collective_id=0, has_side_effects=True, vmem_limit_bytes=60 * 2**20
        ),
    )(orbitals.reshape(tiled), occupations, accumulated.reshape(tiled), right_mat, left_mat)
    return result.reshape(orbitals.shape)


def solution(mesh):
    in_specs = (P("band", "slab", None, None), P("band"), P("band", "slab", None, None))
    out_specs = P("band", "slab", None, None)
    return jax.shard_map(body, mesh=mesh, in_specs=in_specs, out_specs=out_specs, check_vma=False)
```

```python
import functools
import math

import jax
import jax.numpy as jnp
import ml_dtypes
import numpy as np
from jax import lax
from jax.experimental import pallas as pl
from jax.experimental.pallas import tpu as pltpu
from jax.sharding import PartitionSpec as P

MESH = pl.DeviceIdType.MESH
F32 = jnp.float32
BF16 = jnp.bfloat16
SUB = 8

CHUNKS = 4

IN_PV, IN_PR0, IN_PR1, IN_OCC, IN_CV, IN_R = range(6)
IN_VF, IN_T, IN_U, IN_RET, OUT_Q, IN_ACC, IN_MAT, OUT_CHAIN = 6, 9, 12, 15, 17, 18, 19, 20
IN_VD = 21
IN_Q = IN_VD + 3 * CHUNKS


def hartley(extent):
    index = np.arange(extent)
    angle = (index[:, None] * index[None, :] % extent) * (2.0 * math.pi / extent)
    full = np.cos(angle) + np.sin(angle)
    high = full.astype(ml_dtypes.bfloat16)
    low = (full - high.astype(np.float64)).astype(ml_dtypes.bfloat16)
    return high, low


def split(value):
    high = value.astype(BF16)
    low = (value - high.astype(F32)).astype(BF16)
    return high, low


def rows_times(value, matrix):
    n = value.shape[1]
    both = jnp.concatenate(split(value), axis=1)
    out = jnp.dot(both, matrix, preferred_element_type=F32)
    return out[:, :n] + out[:, n:]


def times_columns(matrix, value):
    n = value.shape[0]
    both = jnp.concatenate(split(value), axis=0)
    out = jnp.dot(matrix, both, preferred_element_type=F32)
    return out[:n] + out[n:]


def kernel(
    bands, extent,
    orb, occ, acc_hbm, right_hbm, left_hbm, out,
    acc, right_mat, left_mat, pv, pr0, pr1, occ_own, occ_all, cv, res, vis, mid, fwd, tin, tout, back, done, ret_z, ret,
    send_sem, in_sem, turn,
):
    nz, nw = 2 * bands, bands
    b, s = lax.axis_index("band"), lax.axis_index("slab")
    z, yh, g = s // 2, s % 2, b % 2
    w = (b // 2) * 2 + yh
    place = 2 * w + g

    def device(tw, tg, tz):
        return {"band": (tw // 2) * 2 + tg, "slab": 2 * tz + tw % 2}

    def push(src, dst, sem, target, leave=None):
        pltpu.make_async_remote_copy(
            src_ref=src, dst_ref=dst, recv_sem=in_sem.at[sem],
            send_sem=send_sem.at[sem if leave is None else leave],
            device_id=target, device_id_type=MESH,
        ).start()

    def keep(src, dst, sem):
        pltpu.make_async_copy(src, dst, in_sem.at[sem]).start()

    def arrived(ref, sem):
        pltpu.make_async_copy(ref, ref, in_sem.at[sem]).wait()

    def sent(ref, sem):
        pltpu.make_async_copy(ref, ref, send_sem.at[sem]).wait()

    def loop(low, high, fn):
        def step(i, carry):
            fn(i)
            return carry
        lax.fori_loop(low, high, step, 0)

    keep(acc_hbm, acc, IN_ACC)
    keep(right_hbm, right_mat, IN_MAT)
    keep(left_hbm, left_mat, IN_MAT)
    occ_own[...] = jnp.full(occ_own.shape, occ[0], F32)

    barrier = pltpu.get_barrier_semaphore()

    def greet(target):
        pl.semaphore_signal(barrier, inc=1, device_id=target, device_id_type=MESH)

    def greet_plane(d):
        t = (place + d) % (2 * nw)
        greet(device(t // 2, t % 2, z))

    def far_first(m):
        reach = nz // 2 - m // 2
        return (z + jnp.where(m % 2 == 1, reach, nz - reach)) % nz

    loop(1, nz, lambda m: greet(device(w, g, far_first(m))))
    loop(1, 2 * nw, greet_plane)

    @pl.when(g == 0)
    def _():
        greet(device(w, 1, (z + 1) % nz))

    pl.semaphore_wait(barrier, 2 * nw - 1 + nz - 1 + g)

    mine = 2 * b + yh

    def visitors_out(d):
        t = (place + d) % (2 * nw)
        push(orb.at[0, t % 2, t // 2], pv.at[mine], IN_PV, device(t // 2, t % 2, z))

    def residents_out(d):
        t = (place + d) % (2 * nw)
        tw, tg = t // 2, t % 2
        push(orb.at[2 + tg, :, tw], pr0.at[mine], IN_PR0, device(tw, tg, z))

    def seconds_out(d):
        tw = (w + d) % nw
        push(orb.at[1, :, tw], pr1.at[mine], IN_PR1, device(tw, 1, z))

    def weights_out(d):
        t = (place + d) % (2 * nw)
        tw, tg = t // 2, t % 2

        @pl.when(tw % 2 == yh)
        def _():
            push(occ_own, occ_all.at[b], IN_OCC, device(tw, tg, z))

    loop(1, 2 * nw, visitors_out)
    keep(orb.at[0, g, w], pv.at[mine], IN_PV)
    loop(1, 2 * nw, residents_out)
    keep(orb.at[2 + g, :, w], pr0.at[mine], IN_PR0)

    half = bands // 2

    def signed(m):
        reach = half - (m + 1) // 2
        return jnp.where(m % 2 == 0, reach, -reach)

    def centre_out(m):
        tz = (z // 2 * 2 + 2 * signed(m) + nz) % nz
        owner = (tz // 2 - 2 + bands) % bands
        src, dst = pv.at[pl.ds(2 * owner, 2)], cv.at[pl.ds(2 * z, 2)]

        @pl.when(tz == z)
        def _():
            keep(src, dst, IN_CV)

        @pl.when(tz != z)
        def _():
            push(src, dst, IN_CV, device(w, g, tz))

    def home_out(m, stage, odd):
        tz = (z // 2 * 2 + 2 * signed(m) + odd + nz) % nz
        owner = tz // 2
        src, dst = stage.at[pl.ds(2 * owner, 2)], res.at[pl.ds(2 * z, 2)]

        @pl.when(tz == z)
        def _():
            keep(src, dst, IN_R)

        @pl.when(tz != z)
        def _():
            push(src, dst, IN_R, device(w, g, tz))

    arrived(pv, IN_PV)
    loop(0, bands, centre_out)

    loop(1, nw, seconds_out)

    @pl.when(g == 0)
    def _():
        push(orb.at[1, :, w], pr1.at[mine], IN_PR1, device(w, 1, z))

    @pl.when(g == 1)
    def _():
        keep(orb.at[1, :, w], pr1.at[mine], IN_PR1)

    loop(1, 2 * nw, weights_out)
    keep(occ_own, occ_all.at[b], IN_OCC)

    even = z % 2 == 0
    above, below = device(w, g, (z + 1) % nz), device(w, g, (z - 1 + nz) % nz)
    piece = 2 * nz // CHUNKS

    def visitor(h, k):
        return vis.at[h, pl.ds(piece * k, piece), g]

    def pass_on(src, h, k, target):
        push(src, visitor(h, k), IN_VD + CHUNKS * h + k, target, OUT_CHAIN)

    def came(h, k):
        arrived(visitor(h, k), IN_VD + CHUNKS * h + k)

    sent(pv.at[pl.ds(0, 2 * bands - 2)], IN_CV)

    @pl.when(even)
    def _():
        arrived(cv, IN_CV)
        for k in range(CHUNKS):
            part = cv.at[pl.ds(piece * k, piece)]
            pass_on(part, 1, k, above)
            pass_on(part, 0, k, below)
        for k in range(CHUNKS):
            keep(cv.at[pl.ds(piece * k, piece)], visitor(1, k), IN_VD + CHUNKS + k)

    @pl.when(jnp.logical_not(even))
    def _():
        sent(pv.at[pl.ds(0, 2)], IN_CV)

    @pl.when(g == 0)
    def _():
        arrived(pr0, IN_PR0)
        loop(0, bands, lambda m: home_out(m, pr0, 0))

    @pl.when(even)
    def _():
        for k in range(CHUNKS):
            came(0, k)
            push(
                visitor(0, k), res.at[pl.ds(piece * k, piece), g], IN_R,
                device(w, 0, (z - 1 + nz) % nz), OUT_CHAIN,
            )
            came(2, k)
            pass_on(visitor(2, k), 2, k, above)
        for k in range(CHUNKS):
            came(1, k)

    @pl.when(jnp.logical_not(even))
    def _():
        for k in range(CHUNKS):
            came(0, k)
            pass_on(visitor(0, k), 0, k, below)
            came(1, k)
            pass_on(visitor(1, k), 2, k, above)

    @pl.when(jnp.logical_not(even))
    def _():
        for k in range(CHUNKS):
            came(2, k)

    order = (1, 0, 2)

    def share(h):
        half_vis = vis.at[h, :, g]
        push(half_vis, half_vis, IN_VF + h, device(w, 1 - g, z))

    def transform_x(src, dst):
        for y in range(0, SUB, 2):
            two = jnp.concatenate(
                [src[pl.ds(y + k, extent, stride=SUB), :] for k in range(2)], axis=1
            )
            two = times_columns(left_mat[...], two)
            for k in range(2):
                dst[pl.ds(y + k, extent, stride=SUB), :] = two[:, k * extent:(k + 1) * extent]

    rows = extent * SUB
    slab_rows = SUB * SUB
    for h in order:
        share(h)

    @pl.when(g == 0)
    def _():
        sent(res.at[pl.ds(0, 2 * bands - 2)], IN_R)

        @pl.when(jnp.logical_not(even))
        def _():
            sent(res.at[pl.ds(0, 2)], IN_R)

        pl.semaphore_signal(turn, inc=1, device_id=device(w, 1, z), device_id_type=MESH)

    @pl.when(g == 1)
    def _():
        arrived(pr0, IN_PR0)
        arrived(pr1, IN_PR1)
        pl.semaphore_wait(turn, 1)
        loop(0, bands, lambda m: home_out(m, pr0, 0))
        loop(0, bands, lambda m: home_out(m, pr1, 1))

    arrived(right_mat, IN_MAT)
    arrived(left_mat, IN_MAT)
    arrived(res, IN_R)
    for h in order:
        arrived(vis.at[h, :, 1 - g], IN_VF + h)
        pair = (res[...] * vis[h]).reshape(rows, extent)
        mid[...] = rows_times(pair, right_mat[...])
        transform_x(mid, fwd.at[h])

        def fwd_out(d, h=h):
            tw = (w + d) % nw
            push(fwd.at[h, pl.ds(slab_rows * tw, slab_rows)], tin.at[h, w], IN_T + h, device(tw, g, z))

        loop(1, nw, fwd_out)
        keep(fwd.at[h, pl.ds(slab_rows * w, slab_rows)], tin.at[h, w], IN_T + h)

    def wave(index):
        near = jnp.where(index < extent // 2, index, index - extent)
        return near.astype(F32) * (2.0 * math.pi / extent)

    shape = (extent, extent)
    square = (
        wave(lax.broadcasted_iota(jnp.int32, shape, 0)) ** 2
        + wave(lax.broadcasted_iota(jnp.int32, shape, 1)) ** 2
    )

    def screening(a):
        index = SUB * w + a
        return (4.0 * math.pi / float(extent**3)) / (square + wave(index) ** 2 + 0.01)

    for h in order:
        arrived(tin.at[h], IN_T + h)
        for a in range(0, SUB, 2):
            two = jnp.concatenate(
                [tin[h, :, SUB * (a + k):SUB * (a + k + 1), :].reshape(shape) for k in range(2)],
                axis=1,
            )
            two = times_columns(left_mat[...], two)
            two = two * jnp.concatenate([screening(a), screening(a + 1)], axis=1)
            two = times_columns(left_mat[...], two)
            for k in range(2):
                tout[h, :, SUB * (a + k):SUB * (a + k + 1), :] = two[
                    :, k * extent:(k + 1) * extent
                ].reshape(nw, SUB, extent)

        def back_out(d, h=h):
            tw = (w + d) % nw
            push(tout.at[h, tw], back.at[h, pl.ds(slab_rows * w, slab_rows)], IN_U + h, device(tw, g, z))

        loop(1, nw, back_out)
        keep(tout.at[h, w], back.at[h, pl.ds(slab_rows * w, slab_rows)], IN_U + h)

    arrived(occ_all, IN_OCC)
    for h in order:
        arrived(back.at[h], IN_U + h)
        transform_x(back.at[h], mid)
        potential = rows_times(mid[...], right_mat[...]).reshape(extent // 2, 2, SUB, extent)
        owner = (z // 2 - (h + 1) + bands) % bands
        term = vis[h] * potential * occ_all[owner][None, None]
        term = term.reshape(done.shape)
        if h == order[0]:
            done[...] = term
        else:
            done[...] += term

    def slabs_out(m):
        tz = far_first(m)
        push(done.at[tz], ret_z.at[z // 2, z % 2], IN_Q + z // 2, device(w, g, tz), OUT_Q)

    loop(1, nz, slabs_out)
    keep(done.at[z], ret_z.at[z // 2, z % 2], IN_Q + z // 2)

    def owner_out(m):
        owner = (z // 2 + signed(m) + bands) % bands
        arrived(ret_z.at[owner], IN_Q + owner)
        dst = ret.at[:, g, :, w]
        for part in range(2):
            src = ret_z.at[owner, :, part]
            here = jnp.logical_and(owner == b, yh == part)

            @pl.when(here)
            def _():
                keep(src, dst, IN_RET + g)

            @pl.when(jnp.logical_not(here))
            def _():
                target = {"band": owner, "slab": 2 * z + part}
                push(src, dst, IN_RET + g, target, IN_RET)

    loop(0, bands, owner_out)
    arrived(acc, IN_ACC)
    for core in range(2):
        arrived(ret.at[:, core], IN_RET + core)
        for first in range(2):
            j = 2 * (1 - first) + core
            out[j] = acc[j] - ret[first, core]

    sent(pv.at[pl.ds(1, 2 * nw - 1)], IN_PV)
    sent(pr0.at[pl.ds(1, 2 * nw - 1)], IN_PR0)
    sent(pr1.at[pl.ds(0, nw - 1)], IN_PR1)

    @pl.when(g == 0)
    def _():
        sent(pr1.at[0], IN_PR1)

    sent(occ_all.at[pl.ds(0, nw - 1)], IN_OCC)

    @pl.when(g == 1)
    def _():
        sent(res.at[pl.ds(0, 2 * bands - 1)], IN_R)
        sent(res.at[pl.ds(0, 2 * bands - 1)], IN_R)

    sent(cv, OUT_CHAIN)
    sent(cv, OUT_CHAIN)

    @pl.when(even)
    def _():
        sent(cv, OUT_CHAIN)
        sent(cv, OUT_CHAIN)

    for h in order:
        sent(vis.at[h, :, g], IN_VF + h)
        sent(tin.at[h, pl.ds(0, nw - 1)], IN_T + h)
        sent(tout.at[h, pl.ds(0, nw - 1)], IN_U + h)
    sent(done.at[pl.ds(0, nz - 1)], OUT_Q)
    sent(done.at[pl.ds(0, 2 * nw - 1)], IN_RET)


def body(orbitals, occupations, accumulated):
    extent = orbitals.shape[2]
    bands = lax.axis_size("band")
    nz, nw = 2 * bands, bands
    high, low = hartley(extent)
    right_mat = jnp.asarray(np.block([[high, low], [high, low]]))
    left_mat = jnp.asarray(np.block([[high, high], [low, low]]))
    tiled = (orbitals.shape[0], orbitals.shape[1], nw, SUB, extent)
    rows = extent * SUB
    tile = (SUB, extent)
    vmem = pl.BlockSpec(memory_space=pltpu.VMEM)
    hbm = pl.BlockSpec(memory_space=pltpu.HBM)
    scratch = [
        (2 * bands, *tile),
        (2 * bands, 2, *tile),
        (2 * bands, 2, *tile),
        tile,
        (bands, *tile),
        (2 * nz, *tile),
        (2 * nz, 2, *tile),
        (3, 2 * nz, 2, *tile),
        (rows, extent),
        (3, rows, extent),
        (3, nw, SUB * SUB, extent),
        (3, nw, SUB * SUB, extent),
        (3, rows, extent),
        (nz, 2, 2, *tile),
        (bands, 2, 2, 2, *tile),
        (2, 2, 2, nw, *tile),
    ]
    result = pl.pallas_call(
        functools.partial(kernel, bands, extent),
        out_shape=jax.ShapeDtypeStruct(tiled, F32),
        in_specs=[hbm, pl.BlockSpec(memory_space=pltpu.SMEM), hbm, hbm, hbm],
        out_specs=vmem,
        scratch_shapes=[pltpu.VMEM(tiled, F32)]
        + [pltpu.VMEM((2 * extent, 2 * extent), BF16)] * 2
        + [pltpu.VMEM(shape, F32) for shape in scratch]
        + [pltpu.SemaphoreType.DMA((IN_Q + bands,))] * 2
        + [pltpu.SemaphoreType.REGULAR],
        compiler_params=pltpu.CompilerParams(
            collective_id=0, has_side_effects=True, vmem_limit_bytes=60 * 2**20
        ),
    )(orbitals.reshape(tiled), occupations, accumulated.reshape(tiled), right_mat, left_mat)
    return result.reshape(orbitals.shape)


def solution(mesh):
    in_specs = (P("band", "slab", None, None), P("band"), P("band", "slab", None, None))
    out_specs = P("band", "slab", None, None)
    return jax.shard_map(body, mesh=mesh, in_specs=in_specs, out_specs=out_specs, check_vma=False)
```

```python
import functools
import math

import jax
import jax.numpy as jnp
import ml_dtypes
import numpy as np
from jax import lax
from jax.experimental import pallas as pl
from jax.experimental.pallas import tpu as pltpu
from jax.sharding import PartitionSpec as P

MESH = pl.DeviceIdType.MESH
F32 = jnp.float32
BF16 = jnp.bfloat16
SUB = 8

CHUNKS = 8

IN_PV, IN_PR0, IN_PR1, IN_OCC, IN_CV, IN_R = range(6)
IN_VF, IN_T, IN_U, IN_RET, OUT_Q, IN_ACC, IN_MAT, OUT_CHAIN = 6, 9, 12, 15, 17, 18, 19, 20
IN_VD = 21
IN_Q = IN_VD + 3 * CHUNKS


def hartley(extent):
    index = np.arange(extent)
    angle = (index[:, None] * index[None, :] % extent) * (2.0 * math.pi / extent)
    full = np.cos(angle) + np.sin(angle)
    high = full.astype(ml_dtypes.bfloat16)
    low = (full - high.astype(np.float64)).astype(ml_dtypes.bfloat16)
    return high, low


def split(value):
    high = value.astype(BF16)
    low = (value - high.astype(F32)).astype(BF16)
    return high, low


def rows_times(value, matrix):
    n = value.shape[1]
    both = jnp.concatenate(split(value), axis=1)
    out = jnp.dot(both, matrix, preferred_element_type=F32)
    return out[:, :n] + out[:, n:]


def times_columns(matrix, value):
    n = value.shape[0]
    both = jnp.concatenate(split(value), axis=0)
    out = jnp.dot(matrix, both, preferred_element_type=F32)
    return out[:n] + out[n:]


def kernel(
    bands, extent,
    orb, occ, acc_hbm, right_hbm, left_hbm, out,
    acc, right_mat, left_mat, pv, pr0, pr1, occ_own, occ_all, cv, res, vis, mid, fwd, tin, tout, back, done, ret_z, ret,
    send_sem, in_sem, turn,
):
    nz, nw = 2 * bands, bands
    b, s = lax.axis_index("band"), lax.axis_index("slab")
    z, yh, g = s // 2, s % 2, b % 2
    w = (b // 2) * 2 + yh
    place = 2 * w + g

    def device(tw, tg, tz):
        return {"band": (tw // 2) * 2 + tg, "slab": 2 * tz + tw % 2}

    def push(src, dst, sem, target, leave=None):
        pltpu.make_async_remote_copy(
            src_ref=src, dst_ref=dst, recv_sem=in_sem.at[sem],
            send_sem=send_sem.at[sem if leave is None else leave],
            device_id=target, device_id_type=MESH,
        ).start()

    def keep(src, dst, sem):
        pltpu.make_async_copy(src, dst, in_sem.at[sem]).start()

    def arrived(ref, sem):
        pltpu.make_async_copy(ref, ref, in_sem.at[sem]).wait()

    def sent(ref, sem):
        pltpu.make_async_copy(ref, ref, send_sem.at[sem]).wait()

    def loop(low, high, fn):
        def step(i, carry):
            fn(i)
            return carry
        lax.fori_loop(low, high, step, 0)

    keep(acc_hbm, acc, IN_ACC)
    keep(right_hbm, right_mat, IN_MAT)
    keep(left_hbm, left_mat, IN_MAT)
    occ_own[...] = jnp.full(occ_own.shape, occ[0], F32)

    barrier = pltpu.get_barrier_semaphore()

    def greet(target):
        pl.semaphore_signal(barrier, inc=1, device_id=target, device_id_type=MESH)

    def greet_plane(d):
        t = (place + d) % (2 * nw)
        greet(device(t // 2, t % 2, z))

    def far_first(m):
        reach = nz // 2 - m // 2
        return (z + jnp.where(m % 2 == 1, reach, nz - reach)) % nz

    loop(1, nz, lambda m: greet(device(w, g, far_first(m))))
    loop(1, 2 * nw, greet_plane)

    @pl.when(g == 0)
    def _():
        greet(device(w, 1, (z + 1) % nz))

    pl.semaphore_wait(barrier, 2 * nw - 1 + nz - 1 + g)

    mine = 2 * b + yh

    def visitors_out(d):
        t = (place + d) % (2 * nw)
        push(orb.at[0, t % 2, t // 2], pv.at[mine], IN_PV, device(t // 2, t % 2, z))

    def residents_out(d):
        t = (place + d) % (2 * nw)
        tw, tg = t // 2, t % 2
        push(orb.at[2 + tg, :, tw], pr0.at[mine], IN_PR0, device(tw, tg, z))

    def seconds_out(d):
        tw = (w + d) % nw
        push(orb.at[1, :, tw], pr1.at[mine], IN_PR1, device(tw, 1, z))

    def weights_out(d):
        t = (place + d) % (2 * nw)
        tw, tg = t // 2, t % 2

        @pl.when(tw % 2 == yh)
        def _():
            push(occ_own, occ_all.at[b], IN_OCC, device(tw, tg, z))

    loop(1, 2 * nw, visitors_out)
    keep(orb.at[0, g, w], pv.at[mine], IN_PV)
    loop(1, 2 * nw, residents_out)
    keep(orb.at[2 + g, :, w], pr0.at[mine], IN_PR0)

    half = bands // 2

    def signed(m):
        reach = half - (m + 1) // 2
        return jnp.where(m % 2 == 0, reach, -reach)

    def centre_out(m):
        tz = (z // 2 * 2 + 2 * signed(m) + nz) % nz
        owner = (tz // 2 - 2 + bands) % bands
        src, dst = pv.at[pl.ds(2 * owner, 2)], cv.at[pl.ds(2 * z, 2)]

        @pl.when(tz == z)
        def _():
            keep(src, dst, IN_CV)

        @pl.when(tz != z)
        def _():
            push(src, dst, IN_CV, device(w, g, tz))

    def home_out(m, stage, odd):
        tz = (z // 2 * 2 + 2 * signed(m) + odd + nz) % nz
        owner = tz // 2
        src, dst = stage.at[pl.ds(2 * owner, 2)], res.at[pl.ds(2 * z, 2)]

        @pl.when(tz == z)
        def _():
            keep(src, dst, IN_R)

        @pl.when(tz != z)
        def _():
            push(src, dst, IN_R, device(w, g, tz))

    arrived(pv, IN_PV)
    loop(0, bands, centre_out)

    loop(1, nw, seconds_out)

    @pl.when(g == 0)
    def _():
        push(orb.at[1, :, w], pr1.at[mine], IN_PR1, device(w, 1, z))

    @pl.when(g == 1)
    def _():
        keep(orb.at[1, :, w], pr1.at[mine], IN_PR1)

    loop(1, 2 * nw, weights_out)
    keep(occ_own, occ_all.at[b], IN_OCC)

    even = z % 2 == 0
    above, below = device(w, g, (z + 1) % nz), device(w, g, (z - 1 + nz) % nz)
    piece = 2 * nz // CHUNKS

    def visitor(h, k):
        return vis.at[h, pl.ds(piece * k, piece), g]

    def pass_on(src, h, k, target):
        push(src, visitor(h, k), IN_VD + CHUNKS * h + k, target, OUT_CHAIN)

    def came(h, k):
        arrived(visitor(h, k), IN_VD + CHUNKS * h + k)

    sent(pv.at[pl.ds(0, 2 * bands - 2)], IN_CV)

    @pl.when(even)
    def _():
        arrived(cv, IN_CV)
        for k in range(CHUNKS):
            part = cv.at[pl.ds(piece * k, piece)]
            pass_on(part, 1, k, above)
            pass_on(part, 0, k, below)
        for k in range(CHUNKS):
            keep(cv.at[pl.ds(piece * k, piece)], visitor(1, k), IN_VD + CHUNKS + k)

    @pl.when(jnp.logical_not(even))
    def _():
        sent(pv.at[pl.ds(0, 2)], IN_CV)

    @pl.when(g == 0)
    def _():
        arrived(pr0, IN_PR0)
        loop(0, bands, lambda m: home_out(m, pr0, 0))

    @pl.when(even)
    def _():
        for k in range(CHUNKS):
            came(0, k)
            push(
                visitor(0, k), res.at[pl.ds(piece * k, piece), g], IN_R,
                device(w, 0, (z - 1 + nz) % nz), OUT_CHAIN,
            )
            came(2, k)
            pass_on(visitor(2, k), 2, k, above)
        for k in range(CHUNKS):
            came(1, k)

    @pl.when(jnp.logical_not(even))
    def _():
        for k in range(CHUNKS):
            came(0, k)
            pass_on(visitor(0, k), 0, k, below)
            came(1, k)
            pass_on(visitor(1, k), 2, k, above)

    @pl.when(jnp.logical_not(even))
    def _():
        for k in range(CHUNKS):
            came(2, k)

    order = (1, 0, 2)

    def share(h):
        half_vis = vis.at[h, :, g]
        push(half_vis, half_vis, IN_VF + h, device(w, 1 - g, z))

    def transform_x(src, dst):
        for y in range(0, SUB, 2):
            two = jnp.concatenate(
                [src[pl.ds(y + k, extent, stride=SUB), :] for k in range(2)], axis=1
            )
            two = times_columns(left_mat[...], two)
            for k in range(2):
                dst[pl.ds(y + k, extent, stride=SUB), :] = two[:, k * extent:(k + 1) * extent]

    rows = extent * SUB
    slab_rows = SUB * SUB
    for h in order:
        share(h)

    @pl.when(g == 0)
    def _():
        sent(res.at[pl.ds(0, 2 * bands - 2)], IN_R)

        @pl.when(jnp.logical_not(even))
        def _():
            sent(res.at[pl.ds(0, 2)], IN_R)

        pl.semaphore_signal(turn, inc=1, device_id=device(w, 1, z), device_id_type=MESH)

    @pl.when(g == 1)
    def _():
        arrived(pr0, IN_PR0)
        arrived(pr1, IN_PR1)
        pl.semaphore_wait(turn, 1)
        loop(0, bands, lambda m: home_out(m, pr0, 0))
        loop(0, bands, lambda m: home_out(m, pr1, 1))

    arrived(right_mat, IN_MAT)
    arrived(left_mat, IN_MAT)
    arrived(res, IN_R)
    for h in order:
        arrived(vis.at[h, :, 1 - g], IN_VF + h)
        pair = (res[...] * vis[h]).reshape(rows, extent)
        mid[...] = rows_times(pair, right_mat[...])
        transform_x(mid, fwd.at[h])

        def fwd_out(d, h=h):
            tw = (w + d) % nw
            push(fwd.at[h, pl.ds(slab_rows * tw, slab_rows)], tin.at[h, w], IN_T + h, device(tw, g, z))

        loop(1, nw, fwd_out)
        keep(fwd.at[h, pl.ds(slab_rows * w, slab_rows)], tin.at[h, w], IN_T + h)

    def wave(index):
        near = jnp.where(index < extent // 2, index, index - extent)
        return near.astype(F32) * (2.0 * math.pi / extent)

    shape = (extent, extent)
    square = (
        wave(lax.broadcasted_iota(jnp.int32, shape, 0)) ** 2
        + wave(lax.broadcasted_iota(jnp.int32, shape, 1)) ** 2
    )

    def screening(a):
        index = SUB * w + a
        return (4.0 * math.pi / float(extent**3)) / (square + wave(index) ** 2 + 0.01)

    for h in order:
        arrived(tin.at[h], IN_T + h)
        for a in range(0, SUB, 2):
            two = jnp.concatenate(
                [tin[h, :, SUB * (a + k):SUB * (a + k + 1), :].reshape(shape) for k in range(2)],
                axis=1,
            )
            two = times_columns(left_mat[...], two)
            two = two * jnp.concatenate([screening(a), screening(a + 1)], axis=1)
            two = times_columns(left_mat[...], two)
            for k in range(2):
                tout[h, :, SUB * (a + k):SUB * (a + k + 1), :] = two[
                    :, k * extent:(k + 1) * extent
                ].reshape(nw, SUB, extent)

        def back_out(d, h=h):
            tw = (w + d) % nw
            push(tout.at[h, tw], back.at[h, pl.ds(slab_rows * w, slab_rows)], IN_U + h, device(tw, g, z))

        loop(1, nw, back_out)
        keep(tout.at[h, w], back.at[h, pl.ds(slab_rows * w, slab_rows)], IN_U + h)

    arrived(occ_all, IN_OCC)
    for h in order:
        arrived(back.at[h], IN_U + h)
        transform_x(back.at[h], mid)
        potential = rows_times(mid[...], right_mat[...]).reshape(extent // 2, 2, SUB, extent)
        owner = (z // 2 - (h + 1) + bands) % bands
        term = vis[h] * potential * occ_all[owner][None, None]
        term = term.reshape(done.shape)
        if h == order[0]:
            done[...] = term
        else:
            done[...] += term

    def slabs_out(m):
        tz = far_first(m)
        push(done.at[tz], ret_z.at[z // 2, z % 2], IN_Q + z // 2, device(w, g, tz), OUT_Q)

    loop(1, nz, slabs_out)
    keep(done.at[z], ret_z.at[z // 2, z % 2], IN_Q + z // 2)

    def owner_out(m):
        owner = (z // 2 + signed(m) + bands) % bands
        arrived(ret_z.at[owner], IN_Q + owner)
        dst = ret.at[:, g, :, w]
        for part in range(2):
            src = ret_z.at[owner, :, part]
            here = jnp.logical_and(owner == b, yh == part)

            @pl.when(here)
            def _():
                keep(src, dst, IN_RET + g)

            @pl.when(jnp.logical_not(here))
            def _():
                target = {"band": owner, "slab": 2 * z + part}
                push(src, dst, IN_RET + g, target, IN_RET)

    loop(0, bands, owner_out)
    arrived(acc, IN_ACC)
    for core in range(2):
        arrived(ret.at[:, core], IN_RET + core)
        for first in range(2):
            j = 2 * (1 - first) + core
            out[j] = acc[j] - ret[first, core]

    sent(pv.at[pl.ds(1, 2 * nw - 1)], IN_PV)
    sent(pr0.at[pl.ds(1, 2 * nw - 1)], IN_PR0)
    sent(pr1.at[pl.ds(0, nw - 1)], IN_PR1)

    @pl.when(g == 0)
    def _():
        sent(pr1.at[0], IN_PR1)

    sent(occ_all.at[pl.ds(0, nw - 1)], IN_OCC)

    @pl.when(g == 1)
    def _():
        sent(res.at[pl.ds(0, 2 * bands - 1)], IN_R)
        sent(res.at[pl.ds(0, 2 * bands - 1)], IN_R)

    sent(cv, OUT_CHAIN)
    sent(cv, OUT_CHAIN)

    @pl.when(even)
    def _():
        sent(cv, OUT_CHAIN)
        sent(cv, OUT_CHAIN)

    for h in order:
        sent(vis.at[h, :, g], IN_VF + h)
        sent(tin.at[h, pl.ds(0, nw - 1)], IN_T + h)
        sent(tout.at[h, pl.ds(0, nw - 1)], IN_U + h)
    sent(done.at[pl.ds(0, nz - 1)], OUT_Q)
    sent(done.at[pl.ds(0, 2 * nw - 1)], IN_RET)


def body(orbitals, occupations, accumulated):
    extent = orbitals.shape[2]
    bands = lax.axis_size("band")
    nz, nw = 2 * bands, bands
    high, low = hartley(extent)
    right_mat = jnp.asarray(np.block([[high, low], [high, low]]))
    left_mat = jnp.asarray(np.block([[high, high], [low, low]]))
    tiled = (orbitals.shape[0], orbitals.shape[1], nw, SUB, extent)
    rows = extent * SUB
    tile = (SUB, extent)
    vmem = pl.BlockSpec(memory_space=pltpu.VMEM)
    hbm = pl.BlockSpec(memory_space=pltpu.HBM)
    scratch = [
        (2 * bands, *tile),
        (2 * bands, 2, *tile),
        (2 * bands, 2, *tile),
        tile,
        (bands, *tile),
        (2 * nz, *tile),
        (2 * nz, 2, *tile),
        (3, 2 * nz, 2, *tile),
        (rows, extent),
        (3, rows, extent),
        (3, nw, SUB * SUB, extent),
        (3, nw, SUB * SUB, extent),
        (3, rows, extent),
        (nz, 2, 2, *tile),
        (bands, 2, 2, 2, *tile),
        (2, 2, 2, nw, *tile),
    ]
    result = pl.pallas_call(
        functools.partial(kernel, bands, extent),
        out_shape=jax.ShapeDtypeStruct(tiled, F32),
        in_specs=[hbm, pl.BlockSpec(memory_space=pltpu.SMEM), hbm, hbm, hbm],
        out_specs=vmem,
        scratch_shapes=[pltpu.VMEM(tiled, F32)]
        + [pltpu.VMEM((2 * extent, 2 * extent), BF16)] * 2
        + [pltpu.VMEM(shape, F32) for shape in scratch]
        + [pltpu.SemaphoreType.DMA((IN_Q + bands,))] * 2
        + [pltpu.SemaphoreType.REGULAR],
        compiler_params=pltpu.CompilerParams(
            collective_id=0, has_side_effects=True, vmem_limit_bytes=60 * 2**20
        ),
    )(orbitals.reshape(tiled), occupations, accumulated.reshape(tiled), right_mat, left_mat)
    return result.reshape(orbitals.shape)


def solution(mesh):
    in_specs = (P("band", "slab", None, None), P("band"), P("band", "slab", None, None))
    out_specs = P("band", "slab", None, None)
    return jax.shard_map(body, mesh=mesh, in_specs=in_specs, out_specs=out_specs, check_vma=False)
```
